32 devices in a mesh: pair: 8 (over z, y), aux: 4 (over x, core).
Axes of the slice: x: 2, y: 2, z: 4, core: 2. Of those that a mesh axis runs over, the one named last changes fastest.
Arguments:
- amplitudes: bfloat16 [128, 16384], P('pair'), may hold values from -0.059814453 to 0.059814453
- factor_ca: bfloat16 [6400, 16384], P(('pair', 'aux')), may hold values from -0.5 to 0.5
- factor_db: bfloat16 [6400, 16384], P(('pair', 'aux')), may hold values from -0.5 to 0.5
Outputs:
- ladder: bfloat16 [128, 16384], P('pair', 'aux')
The draws below stay inside these ranges and needn't reach their ends.
All inputs are finite; a program needn't handle non-finite values.
Results may differ from the reference program's by a relative error of at most 0.02.
Values may be sent and summed in bfloat16 or wider, within the bound.
A program may use at most 192 MiB of HBM per device.

```python
import jax
import jax.numpy as jnp
from jax import lax

NAUX = 6400
A = 128
B = 128
C = 128
D = 128
NIJ = 128
N_AUX = 4


def levels(key, dims, split, least, largest):
    def one(dim, shards_of):
        steps = jax.random.uniform(jax.random.fold_in(jax.random.fold_in(key, 6), dim), (shards_of,), jnp.float32, least / len(split), largest / len(split))
        return jnp.repeat(jnp.exp(steps), dims[dim] // shards_of).reshape((-1,) + (1,) * (len(dims) - dim - 1))

    gain = one(*split[0])
    for cut in split[1:]:
        gain = gain * one(*cut)
    return gain


def bell_draw(own_key, shape, scale, most, cuts=(), held_as=jnp.bfloat16):
    entries = scale * jax.random.normal(own_key, shape, jnp.float32)
    if cuts:
        entries = entries * levels(own_key, shape, cuts, -0.22, 0.18)
    return jnp.clip(entries, -most, most).astype(held_as)


def setup_inputs(seed: int = 0) -> dict:
    key_of = jax.random.split(jax.random.key(seed), 4)
    amplitudes = bell_draw(key_of[0], (NIJ, C * D), 0.01, 0.059814453, ((0, 8),))
    factor_ca = bell_draw(key_of[1], (NAUX, C * A), 160 ** -0.5, 0.5, ((0, 32),))
    factor_db = bell_draw(key_of[2], (NAUX, D * B), 160 ** -0.5, 0.5, ((0, 32),))
    return dict(amplitudes=amplitudes, factor_ca=factor_ca, factor_db=factor_db)


def reference(amplitudes, factor_ca, factor_db):
    right_flat = factor_db
    amps_flat = amplitudes
    left_cube = factor_ca.reshape(NAUX, C, A)
    quarter = NAUX // N_AUX

    def per_column(panel_col):
        total = jnp.zeros((C, D * B), jnp.float32)
        for block in range(N_AUX):
            left_rows = panel_col[block * quarter:(block + 1) * quarter]
            right_rows = right_flat[block * quarter:(block + 1) * quarter]
            partial_ints = jnp.dot(left_rows.T, right_rows, preferred_element_type=jnp.float32)
            rounded = lax.optimization_barrier(partial_ints.astype(jnp.bfloat16))
            total = total + rounded.astype(jnp.float32)
        ints_a = total.astype(jnp.bfloat16).reshape(C * D, B)
        return jnp.dot(amps_flat, ints_a, preferred_element_type=jnp.float32)

    stacked = lax.map(per_column, jnp.moveaxis(left_cube, 2, 0))
    return jnp.transpose(stacked, (1, 0, 2)).reshape(NIJ, A * B).astype(jnp.bfloat16)
```

```python
import functools

import jax
import jax.numpy as jnp
from jax import lax
from jax.experimental import pallas as pl
from jax.experimental.pallas import tpu as pltpu
from jax.sharding import PartitionSpec as P

A = 128
B = 128
C = 128
D = 128
NA = 8
DC = 8


def ladder_kernel(x_ref, y_ref, t_ref, o_ref, xt, s, acc):
    xt[...] = x_ref[...].T
    acc[...] = jnp.zeros_like(acc)

    @pl.loop(0, D // DC)
    def _(j):
        for dd in range(0, DC, 2):
            cols = pl.ds(pl.multiple_of((j * DC + dd) * B, 2 * B), 2 * B)
            v = jnp.dot(xt[...], y_ref[:, cols], preferred_element_type=jnp.float32)
            v = v.astype(jnp.bfloat16)
            for a in range(NA):
                for e in range(2):
                    s[(dd + e) * C:(dd + e + 1) * C, a * B:(a + 1) * B] = v[
                        a * C:(a + 1) * C, e * B:(e + 1) * B
                    ]
        tc = pl.ds(pl.multiple_of(j * DC * C, DC * C), DC * C)
        acc[...] += jnp.dot(t_ref[:, tc], s[...], preferred_element_type=jnp.float32)

    o_ref[...] = acc[...].astype(jnp.bfloat16)


def partial_ladder(x, y, t):
    rows, a_cols = x.shape
    n_ij = t.shape[0]
    na = a_cols // C
    return pl.pallas_call(
        ladder_kernel,
        grid=(na // NA,),
        in_specs=[
            pl.BlockSpec((rows, NA * C), lambda i: (0, i)),
            pl.BlockSpec((rows, D * B), lambda i: (0, 0), pipeline_mode=pl.Buffered(1)),
            pl.BlockSpec((n_ij, D * C), lambda i: (0, 0), pipeline_mode=pl.Buffered(1)),
        ],
        out_specs=pl.BlockSpec((n_ij, NA * B), lambda i: (0, i)),
        out_shape=jax.ShapeDtypeStruct((n_ij, na * B), jnp.bfloat16),
        scratch_shapes=[
            pltpu.VMEM((NA * C, rows), jnp.bfloat16),
            pltpu.VMEM((DC * C, NA * B), jnp.bfloat16),
            pltpu.VMEM((n_ij, NA * B), jnp.float32),
        ],
        compiler_params=pltpu.CompilerParams(vmem_limit_bytes=56 << 20),
        cost_estimate=pl.CostEstimate(
            flops=2 * na * C * D * B * (rows + n_ij),
            bytes_accessed=2 * rows * (a_cols + D * B),
            transcendentals=0,
        ),
    )(x, y, t)


def local(amplitudes, factor_ca, factor_db):
    n_aux = lax.axis_size("aux")
    n_x = n_aux // 2
    aux = lax.axis_index("aux")
    core = lax.rem(aux, 2)
    chip = aux // 2
    rows = factor_ca.shape[0]
    n_pair_rows = amplitudes.shape[0]
    a_share = A // n_aux
    swap = [(i, i ^ 1) for i in range(n_aux)]

    t_own = amplitudes.reshape(n_pair_rows, C, D).transpose(0, 2, 1).reshape(n_pair_rows, D * C)
    t = lax.all_gather(t_own, "pair", axis=0, tiled=True)

    x_t = factor_ca.reshape(rows, C, A).transpose(0, 2, 1)
    x_t = x_t.reshape(rows, n_x, 2, a_share * C)
    x_mine = lax.dynamic_index_in_dim(x_t, core, 2, keepdims=False).reshape(rows, -1)
    x_give = lax.dynamic_index_in_dim(x_t, 1 - core, 2, keepdims=False).reshape(rows, -1)
    y_other = lax.ppermute(factor_db, "aux", swap)
    x_other = lax.ppermute(x_give, "aux", swap)
    x = jnp.concatenate([x_mine, x_other], axis=0)
    y = jnp.concatenate([factor_db, y_other], axis=0)

    part = partial_ladder(x, y, t)
    n_ij = part.shape[0]
    part = part.reshape(n_ij, n_x, a_share * B)
    total = lax.dynamic_index_in_dim(part, chip, 1, keepdims=False).astype(jnp.float32)
    for k in range(1, n_x):
        give = lax.dynamic_index_in_dim(part, lax.rem(chip + k, n_x), 1, keepdims=False)
        hop = [(i, (i + 2 * k) % n_aux) for i in range(n_aux)]
        total = total + lax.ppermute(give, "aux", hop).astype(jnp.float32)
    return lax.psum_scatter(
        total.astype(jnp.bfloat16), "pair", scatter_dimension=0, tiled=True
    )


def solution(mesh):
    return jax.shard_map(
        local,
        mesh=mesh,
        in_specs=(P("pair", None), P(("pair", "aux"), None), P(("pair", "aux"), None)),
        out_specs=P("pair", "aux"),
        check_vma=False,
    )
```

```python
import functools

import jax
import jax.numpy as jnp
from jax import lax
from jax.experimental import pallas as pl
from jax.experimental.pallas import tpu as pltpu
from jax.sharding import PartitionSpec as P

A = 128
B = 128
C = 128
D = 128
NA = 8
DC = 8
CHUNKS = 4


def ladder_kernel(xo_ref, xn_ref, yo_ref, yn_ref, t_ref, o_ref, xt, y, s, acc):
    rows = xo_ref.shape[0]
    half = y.shape[0] // 2
    n_blocks = y.shape[1] // (DC * B)

    @pl.when(pl.program_id(0) == 0)
    def _():
        if half > rows:
            y[...] = jnp.zeros_like(y)
        y[0:rows, :] = yo_ref[...]
        y[half:half + rows, :] = yn_ref[...]

    if half > rows:
        xt[...] = jnp.zeros_like(xt)
    xt[:, 0:rows] = xo_ref[...].T
    xt[:, half:half + rows] = xn_ref[...].T
    acc[...] = jnp.zeros_like(acc)

    def build(j, slot):
        for dd in range(0, DC, 2):
            cols = pl.ds(pl.multiple_of((j * DC + dd) * B, 2 * B), 2 * B)
            v = jnp.dot(xt[...], y[:, cols], preferred_element_type=jnp.float32)
            v = v.astype(jnp.bfloat16)
            for a in range(NA):
                for e in range(2):
                    s[slot, (dd + e) * C:(dd + e + 1) * C, a * B:(a + 1) * B] = v[
                        a * C:(a + 1) * C, e * B:(e + 1) * B
                    ]

    def contract(j, slot):
        tc = pl.ds(pl.multiple_of(j * DC * C, DC * C), DC * C)
        acc[...] += jnp.dot(t_ref[:, tc], s[slot], preferred_element_type=jnp.float32)

    build(0, 0)

    @pl.loop(0, n_blocks // 2 - 1)
    def _(h):
        build(2 * h + 1, 1)
        contract(2 * h, 0)
        build(2 * h + 2, 0)
        contract(2 * h + 1, 1)

    build(n_blocks - 1, 1)
    contract(n_blocks - 2, 0)
    contract(n_blocks - 1, 1)
    o_ref[0] = acc[...].astype(jnp.bfloat16)


def partial_ladder(xo, xn, yo, yn, t, chunk, n_chunks, n_out):
    rows, x_cols = xo.shape
    y_cols = yo.shape[1]
    n_ij = t.shape[0]
    na = x_cols // C // n_out // n_chunks
    steps = na // NA
    half = -(-rows // 16) * 16
    whole = lambda i: (0, 0)
    one = pl.Buffered(1)

    def x_map(i):
        return (0, (i // steps) * (n_chunks * steps) + chunk * steps + i % steps)

    return pl.pallas_call(
        ladder_kernel,
        grid=(n_out * steps,),
        in_specs=[
            pl.BlockSpec((rows, NA * C), x_map),
            pl.BlockSpec((rows, NA * C), x_map),
            pl.BlockSpec((rows, y_cols), whole, pipeline_mode=one),
            pl.BlockSpec((rows, y_cols), whole, pipeline_mode=one),
            pl.BlockSpec(t.shape, whole, pipeline_mode=one),
        ],
        out_specs=pl.BlockSpec((1, n_ij, NA * B), lambda i: (i // steps, 0, i % steps)),
        out_shape=jax.ShapeDtypeStruct((n_out, n_ij, na * B), jnp.bfloat16),
        scratch_shapes=[
            pltpu.VMEM((NA * C, 2 * half), jnp.bfloat16),
            pltpu.VMEM((2 * half, y_cols), jnp.bfloat16),
            pltpu.VMEM((2, DC * C, NA * B), jnp.bfloat16),
            pltpu.VMEM((n_ij, NA * B), jnp.float32),
        ],
        compiler_params=pltpu.CompilerParams(vmem_limit_bytes=56 << 20),
        cost_estimate=pl.CostEstimate(
            flops=2 * n_out * na * C * y_cols * (2 * rows + n_ij),
            bytes_accessed=4 * rows * (n_out * na * C + y_cols),
            transcendentals=0,
        ),
    )(xo, xn, yo, yn, t)


def local(amplitudes, factor_ca, factor_db):
    n_aux = lax.axis_size("aux")
    aux = lax.axis_index("aux")
    core = lax.rem(aux, 2)
    rows = factor_ca.shape[0]
    n_pair_rows = amplitudes.shape[0]
    d_half = D // 2
    a_share = A // n_aux
    swap = [(i, i ^ 1) for i in range(n_aux)]

    t_own = lax.dynamic_slice_in_dim(
        amplitudes.reshape(n_pair_rows, C, D).transpose(0, 2, 1),
        core * d_half + (aux // 2) * (d_half // 2),
        d_half // 2,
        1,
    ).reshape(n_pair_rows, d_half // 2 * C)
    n_pair = lax.axis_size("pair")
    t_send = jnp.broadcast_to(t_own[None], (n_pair,) + t_own.shape)
    t_first = lax.all_to_all(t_send, "pair", split_axis=0, concat_axis=0, tiled=True)
    t = t_first.reshape(n_pair * n_pair_rows, d_half // 2 * C)
    t_new = lax.ppermute(t, "aux", [(i, i ^ 2) for i in range(n_aux)])
    low = aux // 2 == 0
    t = jnp.concatenate([jnp.where(low, t, t_new), jnp.where(low, t_new, t)], axis=1)

    cols = d_half * B
    y_own = lax.dynamic_slice_in_dim(factor_db, core * cols, cols, 1)
    y_new = lax.ppermute(
        lax.dynamic_slice_in_dim(factor_db, (1 - core) * cols, cols, 1), "aux", swap
    )
    x_own, t_first = lax.optimization_barrier(
        (factor_ca.reshape(rows, C, A).transpose(0, 2, 1), t_first)
    )
    x_own = x_own.reshape(rows, A * C)
    x_new = lax.ppermute(x_own, "aux", swap)

    outs = []
    for chunk in range(CHUNKS):
        part = partial_ladder(x_own, x_new, y_own, y_new, t, chunk, CHUNKS, n_aux)
        total = lax.dynamic_index_in_dim(part, aux, 0, keepdims=False).astype(jnp.float32)
        for k in range(1, n_aux):
            give = lax.dynamic_index_in_dim(part, aux ^ k, 0, keepdims=False)
            hop = [(i, i ^ k) for i in range(n_aux)]
            total = total + lax.ppermute(give, "aux", hop).astype(jnp.float32)
        outs.append(
            lax.all_to_all(
                total.astype(jnp.bfloat16).reshape(n_pair, n_pair_rows, -1),
                "pair",
                split_axis=0,
                concat_axis=0,
                tiled=True,
            ).astype(jnp.float32).sum(0).astype(jnp.bfloat16)
        )
    return jnp.concatenate(outs, axis=1)


def solution(mesh):
    return jax.shard_map(
        local,
        mesh=mesh,
        in_specs=(P("pair", None), P(("pair", "aux"), None), P(("pair", "aux"), None)),
        out_specs=P("pair", "aux"),
        check_vma=False,
    )
```
